32 devices in a mesh: ctx: 8 (over y, x, core), db: 4 (over z).
Axes of the slice: x: 2, y: 2, z: 4, core: 2. Of those that a mesh axis runs over, the one named last changes fastest.
Arguments:
- stream: bfloat16 [3072, 4096], P('ctx', 'db'), may hold values from -6 to 6
- history: bfloat16 [8, 3072, 4096], P(None, 'ctx', 'db'), may hold values from -6 to 6
- dwa_weights: float32 [9], replicated, may hold values from -0.5 to 1
- w_query: bfloat16 [4096, 4096], P('ctx', 'db'), may hold values from -0.09375 to 0.09375
- w_out: bfloat16 [4096, 4096], P('db', 'ctx'), may hold values from -0.125 to 0.125
- encoded_kv: bfloat16 [4, 24, 128, 2, 4096], P('db', None, 'ctx'), may hold values from -340 to 340
- neighbour_ids: int32 [96], replicated, may hold values from 0 to 95, each once
Outputs:
- block_out: bfloat16 [3072, 4096], P('ctx', 'db')
- dense: bfloat16 [3072, 4096], P('ctx', 'db')
The draws below stay inside these ranges and needn't reach their ends.
Inputs may be any that keep to these rules, and one draw needn't show every extreme that they name: `neighbour_ids`: each stored neighbour is named by exactly one slot.
All inputs are finite; a program needn't handle non-finite values.
Results may differ from the reference program's by a relative error of at most 0.014.
The reference program's roundings to bfloat16 on the way count: a program that leaves them out, or rounds other values in their place, can miss the bound.
Values may be sent and summed in bfloat16 or wider, within the bound.
A program may use at most 128 MiB of HBM per device.

```python
import jax
import jax.numpy as jnp
from jax import lax

D = 4096
HDIM = 128
LAYERS = 8
SPAN = 64
NLEN = 128
NNB = 2
TOKENS = 3072
SPANS = 48
NSTORE = 96
GROUPS = 4
NBG = 24
N_DB = 4


def draw_encoded_kv(key, part):
    shape = (GROUPS, NBG, NLEN, 2, D)
    first_key = jax.random.fold_in(key, 0)
    base = jnp.clip(jax.random.normal(first_key, shape, jnp.float32), -6.0, 6.0)
    spread = jnp.ones((GROUPS, NBG, NLEN, 1, 1), jnp.float32)
    factor = jnp.concatenate([2.5 * spread, jnp.ones_like(spread)], axis=3)
    return (base * factor).astype(jnp.bfloat16)


def with_spikes(entries, own_key, source, target, shards_of, factor):
    def block_of(axis_at):
        return (jnp.arange(entries.shape[axis_at]) // (entries.shape[axis_at] // shards_of)).reshape((-1,) + (1,) * (entries.ndim - 1 - axis_at))

    one_side = jax.random.permutation(own_key, shards_of)[block_of(target)]
    other_side = (block_of(target) + shards_of // 2) % shards_of
    return jnp.where((block_of(source) == one_side) | (block_of(source) == other_side), factor * entries, entries)


def steps_of(key, extent, shards, smallest, high):
    level, own = 1.0, jax.random.fold_in(key, 6)
    for position, parts in shards:
        steps = jnp.exp(jax.random.uniform(jax.random.fold_in(own, position), (parts,), jnp.float32, smallest / len(shards), high / len(shards)))
        level = level * jnp.repeat(steps, extent[position] // parts).reshape([-1 if axis == position else 1 for axis in range(len(extent))])
    return level


def noise(key, extent, scale, limit, pieces=(), dtype=jnp.bfloat16):
    values = scale * jax.random.normal(key, extent, jnp.float32)
    if pieces:
        values = values * steps_of(key, extent, pieces, -0.22, 0.18)
    return jnp.clip(values, -limit, limit).astype(dtype)


def heavy_noise(stream_key, shape, deviation, reach, cuts, heavy, dtype=jnp.bfloat16):
    result = deviation * jax.random.normal(stream_key, shape, jnp.float32)
    if cuts:
        result = result * steps_of(stream_key, shape, cuts, -0.22, 0.18)
    return jnp.clip(with_spikes(result, jax.random.fold_in(stream_key, 3), *heavy), -reach, reach).astype(dtype)


def setup_inputs(seed: int = 0) -> dict:
    key_of = jax.random.split(jax.random.key(seed), 8)
    return {
        "stream": noise(key_of[0], (TOKENS, D), 1.0, 6.0, ((0, 8), (1, 4))),
        "history": noise(key_of[1], (LAYERS, TOKENS, D), 1.0, 6.0, ((1, 8), (2, 4))),
        "dwa_weights": jnp.clip(jax.random.uniform(key_of[2], (LAYERS + 1,), jnp.float32, -0.5, 1.0), -0.5, 1.0),
        "w_query": noise(key_of[3], (D, D), D ** -0.5, 0.09375, ((0, 8), (1, 4))),
        "w_out": heavy_noise(key_of[4], (D, D), D ** -0.5, 0.125, ((0, 4), (1, 8)), (0, 1, 8, 2.0)),
        "encoded_kv": draw_encoded_kv(jax.random.fold_in(key_of[7], 71), 0),
        "neighbour_ids": jax.random.permutation(key_of[6], NSTORE).astype(jnp.int32),
    }


def attend_one(span_queries, key_rows, value_rows):
    head_count = D // HDIM
    query_heads = span_queries.astype(jnp.float32).reshape(SPAN, head_count, HDIM)
    key_heads = key_rows.astype(jnp.float32).reshape(NNB * NLEN, head_count, HDIM)
    value_heads = value_rows.astype(jnp.float32).reshape(NNB * NLEN, head_count, HDIM)
    scores = jnp.einsum("qhd,khd->hqk", query_heads, key_heads) * (HDIM ** -0.5)
    row_max = jnp.max(scores, axis=-1, keepdims=True)
    exponent = jnp.exp(scores - row_max)
    weights = (exponent / jnp.sum(exponent, axis=-1, keepdims=True)).astype(jnp.bfloat16)
    mixed = jnp.einsum("hqk,khd->qhd", weights.astype(jnp.float32), value_heads)
    return mixed.astype(jnp.bfloat16).reshape(SPAN, D)


def reference(stream, history, dwa_weights, w_query, w_out, encoded_kv, neighbour_ids):
    queries = jnp.dot(stream, w_query, preferred_element_type=jnp.float32).astype(jnp.bfloat16)
    lead_rows = SPAN - 1
    shifted = jnp.concatenate([queries[lead_rows:], jnp.zeros((lead_rows, D), jnp.bfloat16)], 0)
    shifted = shifted.reshape(SPANS, SPAN, D)
    store = encoded_kv.reshape(NSTORE, NLEN, 2, D)
    span_pairs = neighbour_ids.reshape(SPANS, NNB).astype(jnp.int32)

    def one_span(operands):
        span_queries, span_ids = operands
        rows_kv = jnp.take(store, span_ids, axis=0).reshape(NNB * NLEN, 2, D)
        return attend_one(span_queries, rows_kv[:, 0], rows_kv[:, 1])

    mixed = lax.map(one_span, (shifted, span_pairs)).reshape(TOKENS, D)
    attended = jnp.concatenate([jnp.zeros((lead_rows, D), jnp.bfloat16), mixed[:TOKENS - lead_rows]], 0)
    group_width = D // N_DB
    total = jnp.zeros((TOKENS, D), jnp.float32)
    for group in range(N_DB):
        partial_value = jnp.dot(attended[:, group * group_width:(group + 1) * group_width],
                          w_out[group * group_width:(group + 1) * group_width],
                          preferred_element_type=jnp.float32)
        rounded = lax.optimization_barrier(partial_value.astype(jnp.bfloat16))
        total = total + rounded.astype(jnp.float32)
    block = stream.astype(jnp.float32) + total
    dense = dwa_weights[LAYERS] * block
    for layer in range(LAYERS):
        dense = dense + dwa_weights[layer] * history[layer].astype(jnp.float32)
    return block.astype(jnp.bfloat16), dense.astype(jnp.bfloat16)
```

```python
import functools

import jax
import jax.numpy as jnp
from jax import lax
from jax.experimental import pallas as pl
from jax.experimental.pallas import tpu as pltpu
from jax.sharding import PartitionSpec as P

HDIM = 128
SPAN = 64
NNB = 2
MESH = pl.DeviceIdType.MESH


def shifted(block, axis, distance):
    devices = range(lax.axis_size(axis))
    route = [(i - distance, i) for i in devices if i - distance in devices]
    return lax.ppermute(block, axis, route)


def exchange_kernel(n_ctx, n_db, chunks, ids, kv, out, *scratch):
    stores, outgoing = scratch[:chunks], scratch[chunks : 2 * chunks]
    z_send, z_recv, z_local, c_send, c_recv, c_local = scratch[2 * chunks :]
    c, d = lax.axis_index("ctx"), lax.axis_index("db")
    group_size = kv.shape[1]
    width = stores[0].shape[3]
    heads = width // HDIM
    requests = out.shape[1]
    barrier = pltpu.get_barrier_semaphore()
    for r in range(1, n_db):
        pl.semaphore_signal(barrier, inc=1, device_id=(c, lax.rem(d + r, n_db)), device_id_type=MESH)
    for r in range(1, n_ctx):
        pl.semaphore_signal(barrier, inc=1, device_id=(lax.rem(c + r, n_ctx), d), device_id_type=MESH)
    pl.semaphore_wait(barrier, n_db + n_ctx - 2)

    def columns(owner, k):
        return pl.ds(pl.multiple_of(owner * (width * chunks) + k * width, HDIM), width)

    here = pl.ds(d * group_size, group_size)
    z_copies, z_locals = [], []
    for k in range(chunks):
        row = []
        for r in range(1, n_db):
            peer = lax.rem(d + r, n_db)
            copy = pltpu.make_async_remote_copy(
                src_ref=kv.at[0, :, :, :, columns(peer, k)],
                dst_ref=stores[k].at[here],
                send_sem=z_send.at[k, r],
                recv_sem=z_recv.at[k, r],
                device_id=(c, peer),
                device_id_type=MESH,
            )
            copy.start()
            row.append(copy)
        z_copies.append(row)
        local = pltpu.make_async_copy(
            kv.at[0, :, :, :, columns(d, k)], stores[k].at[here], z_local.at[k]
        )
        local.start()
        z_locals.append(local)
    c_copies = []
    for k in range(chunks):
        z_locals[k].wait()
        for copy in z_copies[k]:
            copy.wait_recv()

        def place(i, carry, k=k):
            block = stores[k][ids[i]]
            to, slot = i // requests, lax.rem(i, requests)
            for h in range(heads):
                outgoing[k][to, h, slot] = block[:, :, h * HDIM : (h + 1) * HDIM]
            return carry

        lax.fori_loop(0, n_ctx * requests, place, 0)
        head_range = pl.ds(k * heads, heads)
        for r in range(1, n_ctx):
            peer = lax.rem(c + r, n_ctx)
            copy = pltpu.make_async_remote_copy(
                src_ref=outgoing[k].at[peer],
                dst_ref=out.at[head_range, :, c],
                send_sem=c_send.at[k, r],
                recv_sem=c_recv.at[k, r],
                device_id=(peer, d),
                device_id_type=MESH,
            )
            copy.start()
            c_copies.append(copy)
        local = pltpu.make_async_copy(
            outgoing[k].at[c], out.at[head_range, :, c], c_local.at[k]
        )
        local.start()
        z_locals.append(local)
    for row in z_copies:
        for copy in row:
            copy.wait_send()
    for local in z_locals[chunks:]:
        local.wait()
    for copy in c_copies:
        copy.wait()


def exchange(encoded_kv, neighbour_ids):
    n_ctx, n_db = lax.axis_size("ctx"), lax.axis_size("db")
    _, group_size, slab, two, full_width = encoded_kv.shape
    local_width = full_width // n_db
    heads = local_width // HDIM
    chunk_heads = 2 if heads % 2 == 0 else 1
    chunks = heads // chunk_heads
    stored = group_size * n_db
    requests = stored // n_ctx
    dtype = encoded_kv.dtype
    dma = pltpu.SemaphoreType.DMA
    return pl.pallas_call(
        functools.partial(exchange_kernel, n_ctx, n_db, chunks),
        out_shape=jax.ShapeDtypeStruct((heads, requests, n_ctx, slab, two, HDIM), dtype),
        in_specs=[
            pl.BlockSpec(memory_space=pltpu.SMEM),
            pl.BlockSpec(memory_space=pl.ANY),
        ],
        out_specs=pl.BlockSpec(memory_space=pl.ANY),
        scratch_shapes=[
            pltpu.VMEM((stored, slab, two, chunk_heads * HDIM), dtype) for _ in range(chunks)
        ]
        + [
            pltpu.VMEM((n_ctx, chunk_heads, requests, slab, two, HDIM), dtype)
            for _ in range(chunks)
        ]
        + [
            dma((chunks, n_db)),
            dma((chunks, n_db)),
            dma((chunks,)),
            dma((chunks, n_ctx)),
            dma((chunks, n_ctx)),
            dma((chunks,)),
        ],
        compiler_params=pltpu.CompilerParams(
            collective_id=0, has_side_effects=True, vmem_limit_bytes=32 * 1024 * 1024
        ),
        name="exchange",
    )(neighbour_ids, encoded_kv)


def attend_kernel(spans, q, kv, out):
    keys = kv.shape[1]
    odd = lax.rem(lax.broadcasted_iota(jnp.int32, (SPAN, keys), 1), 2) == 1
    for s in range(spans):
        rows = slice(s * SPAN, (s + 1) * SPAN)
        pairs = kv[s]
        scores = lax.dot_general(
            q[rows, :], pairs, (((1,), (1,)), ((), ())), preferred_element_type=jnp.float32
        ) * HDIM ** (-0.5)
        scores = jnp.where(odd, -jnp.inf, scores)
        exponent = jnp.exp(scores - jnp.max(scores, axis=-1, keepdims=True))
        weights = exponent / jnp.sum(exponent, axis=-1, keepdims=True)
        moved = pltpu.roll(weights, 1, 1).astype(jnp.bfloat16)
        mixed = jnp.dot(moved, pairs, preferred_element_type=jnp.float32)
        out[rows, :] = mixed.astype(jnp.bfloat16)


def attend(queries, pairs):
    rows, width = queries.shape
    heads, spans, keys, _ = pairs.shape
    return pl.pallas_call(
        functools.partial(attend_kernel, spans),
        grid=(heads,),
        out_shape=jax.ShapeDtypeStruct((rows, width), jnp.bfloat16),
        in_specs=[
            pl.BlockSpec((rows, HDIM), lambda h: (0, h)),
            pl.BlockSpec((None, spans, keys, HDIM), lambda h: (h, 0, 0, 0)),
        ],
        out_specs=pl.BlockSpec((rows, HDIM), lambda h: (0, h)),
        compiler_params=pltpu.CompilerParams(vmem_limit_bytes=32 * 1024 * 1024),
        name="attend",
    )(queries, pairs)


def on_device(stream, history, dwa_weights, w_query, w_out, encoded_kv, neighbour_ids):
    tok_rows = stream.shape[0]
    local_width = w_query.shape[1]
    spans_here = tok_rows // SPAN
    lead_rows = SPAN - 1
    full_stream = lax.all_gather(stream, "db", axis=1, tiled=True)
    queries = jnp.dot(
        full_stream,
        lax.all_gather(w_query, "ctx", axis=0, tiled=True),
        preferred_element_type=jnp.float32,
    ).astype(jnp.bfloat16)
    out_full = lax.all_gather(w_out, "ctx", axis=1, tiled=True)
    arrived = exchange(encoded_kv, neighbour_ids)
    pairs = arrived.reshape(local_width // HDIM, spans_here, -1, HDIM)
    following = shifted(queries[:lead_rows], "ctx", -1)
    grouped = jnp.concatenate([queries[lead_rows:], following], 0)
    mixed = attend(grouped, pairs)
    earlier = shifted(mixed[tok_rows - lead_rows :], "ctx", 1)
    attended = jnp.concatenate([earlier, mixed[: tok_rows - lead_rows]], 0)
    partial_value = jnp.dot(attended, out_full, preferred_element_type=jnp.float32)
    summed = lax.psum_scatter(
        partial_value.astype(jnp.bfloat16), "db", scatter_dimension=1, tiled=True
    ).astype(jnp.float32)
    block = stream.astype(jnp.float32) + summed
    dense = dwa_weights[-1] * block + jnp.sum(
        history.astype(jnp.float32) * dwa_weights[:-1, None, None], axis=0
    )
    return (block.astype(jnp.bfloat16), dense.astype(jnp.bfloat16))


def solution(mesh):
    placed = (
        P("ctx", "db"),
        P(None, "ctx", "db"),
        P(),
        P("ctx", "db"),
        P("db", "ctx"),
        P("db", None, "ctx", None, None),
        P(),
    )
    return jax.shard_map(
        on_device,
        mesh=mesh,
        in_specs=placed,
        out_specs=(P("ctx", "db"), P("ctx", "db")),
        check_vma=False,
    )
```

```python
import functools

import jax
import jax.numpy as jnp
from jax import lax
from jax.experimental import pallas as pl
from jax.experimental.pallas import tpu as pltpu
from jax.sharding import PartitionSpec as P

HDIM = 128
SPAN = 64
NNB = 2
MESH = pl.DeviceIdType.MESH


def shifted(block, axis, distance):
    devices = range(lax.axis_size(axis))
    route = [(i - distance, i) for i in devices if i - distance in devices]
    return lax.ppermute(block, axis, route)


def partner(own, r, count):
    if count & (count - 1):
        return lax.rem(own + r, count)
    bits = [1 << b for b in range(count.bit_length() - 1)]
    return sum(lax.rem(own // bit + (1 if r & bit else 0), 2) * bit for bit in bits)


def exchange_kernel(n_ctx, n_db, chunks, ids, kv, stream, out, full, *scratch):
    stores, outgoing = scratch[:chunks], scratch[chunks : 2 * chunks]
    z_send, z_recv, z_local, c_send, c_recv, c_local, s_send, s_recv, s_local = scratch[2 * chunks :]
    c, d = lax.axis_index("ctx"), lax.axis_index("db")
    group_size = kv.shape[1]
    width = stores[0].shape[3]
    heads = width // HDIM
    requests = out.shape[1]
    barrier = pltpu.get_barrier_semaphore()
    for r in range(1, n_db):
        pl.semaphore_signal(barrier, inc=1, device_id=(c, lax.rem(d + r, n_db)), device_id_type=MESH)
    for r in range(1, n_ctx):
        pl.semaphore_signal(barrier, inc=1, device_id=(lax.rem(c + r, n_ctx), d), device_id_type=MESH)
    pl.semaphore_wait(barrier, n_db + n_ctx - 2)

    def columns(owner, k):
        return pl.ds(pl.multiple_of(owner * (width * chunks) + k * width, HDIM), width)

    own_width = stream.shape[1]

    def block_of(owner):
        return full.at[:, pl.ds(pl.multiple_of(owner * own_width, HDIM), own_width)]

    def passing(step, side, owner):
        return pltpu.make_async_remote_copy(
            src_ref=stream if step == 0 else block_of(owner),
            dst_ref=block_of(owner),
            send_sem=s_send.at[(side + 1) // 2, step],
            recv_sem=s_recv.at[(side + 1) // 2, step],
            device_id=(c, d + side),
            device_id_type=MESH,
        )

    def sends(step, side):
        owner = d - side * step
        return (owner >= 0) & (owner < n_db) & (d + side >= 0) & (d + side < n_db), owner

    def pass_on(step):
        for side in (-1, 1):
            if step > 0:
                take_in(step - 1, side)
            live, owner = sends(step, side)

            @pl.when(live)
            def _(step=step, side=side, owner=owner):
                passing(step, side, owner).start()

    def take_in(step, side):
        owner = d - side * (step + 1)

        @pl.when((owner >= 0) & (owner < n_db))
        def _():
            pltpu.make_async_remote_copy(
                src_ref=block_of(owner),
                dst_ref=block_of(owner),
                send_sem=s_send.at[(side + 1) // 2, step],
                recv_sem=s_recv.at[(side + 1) // 2, step],
                device_id=(c, d - side),
                device_id_type=MESH,
            ).wait_recv()

    own = pltpu.make_async_copy(stream, block_of(d), s_local)
    own.start()
    pass_on(0)
    here = pl.ds(d * group_size, group_size)
    z_copies, z_locals = [], []
    for k in range(chunks):
        row = []
        for r in reversed(range(1, n_db)):
            peer = partner(d, r, n_db)
            copy = pltpu.make_async_remote_copy(
                src_ref=kv.at[0, :, :, :, columns(peer, k)],
                dst_ref=stores[k].at[here],
                send_sem=z_send.at[k, r],
                recv_sem=z_recv.at[k, r],
                device_id=(c, peer),
                device_id_type=MESH,
            )
            copy.start()
            row.append(copy)
        z_copies.append(row)
        local = pltpu.make_async_copy(
            kv.at[0, :, :, :, columns(d, k)], stores[k].at[here], z_local.at[k]
        )
        local.start()
        z_locals.append(local)
    c_copies = []
    steps = list(range(1, n_db - 1))
    for k in range(chunks):
        if steps:
            pass_on(steps.pop(0))
        z_locals[k].wait()
        for copy in z_copies[k]:
            copy.wait_recv()

        def place(i, carry, k=k):
            block = stores[k][ids[i]]
            to, slot = i // requests, lax.rem(i, requests)
            for h in range(heads):
                outgoing[k][to, h, slot] = block[:, :, h * HDIM : (h + 1) * HDIM]
            return carry

        lax.fori_loop(0, n_ctx * requests, place, 0)
        head_range = pl.ds(k * heads, heads)
        for r in range(1, n_ctx):
            peer = lax.rem(c + r, n_ctx)
            copy = pltpu.make_async_remote_copy(
                src_ref=outgoing[k].at[peer],
                dst_ref=out.at[head_range, :, c],
                send_sem=c_send.at[k, r],
                recv_sem=c_recv.at[k, r],
                device_id=(peer, d),
                device_id_type=MESH,
            )
            copy.start()
            c_copies.append(copy)
        local = pltpu.make_async_copy(
            outgoing[k].at[c], out.at[head_range, :, c], c_local.at[k]
        )
        local.start()
        z_locals.append(local)
    for step in steps:
        pass_on(step)
    for side in (-1, 1):
        take_in(n_db - 2, side)
        for step in range(n_db - 1):
            live, owner = sends(step, side)

            @pl.when(live)
            def _(step=step, side=side, owner=owner):
                passing(step, side, owner).wait_send()

    own.wait()
    for row in z_copies:
        for copy in row:
            copy.wait_send()
    for local in z_locals[chunks:]:
        local.wait()
    for copy in c_copies:
        copy.wait()


def exchange(encoded_kv, neighbour_ids, stream):
    n_ctx, n_db = lax.axis_size("ctx"), lax.axis_size("db")
    _, group_size, slab, two, full_width = encoded_kv.shape
    local_width = full_width // n_db
    heads = local_width // HDIM
    chunk_heads = 2 if heads % 2 == 0 else 1
    chunks = heads // chunk_heads
    stored = group_size * n_db
    requests = stored // n_ctx
    dtype = encoded_kv.dtype
    dma = pltpu.SemaphoreType.DMA
    return pl.pallas_call(
        functools.partial(exchange_kernel, n_ctx, n_db, chunks),
        out_shape=(
            jax.ShapeDtypeStruct((heads, requests, n_ctx, slab, two, HDIM), dtype),
            jax.ShapeDtypeStruct((stream.shape[0], full_width), stream.dtype),
        ),
        in_specs=[
            pl.BlockSpec(memory_space=pltpu.SMEM),
            pl.BlockSpec(memory_space=pltpu.HBM),
            pl.BlockSpec(memory_space=pl.ANY),
        ],
        out_specs=(pl.BlockSpec(memory_space=pl.ANY), pl.BlockSpec(memory_space=pl.ANY)),
        scratch_shapes=[
            pltpu.VMEM((stored, slab, two, chunk_heads * HDIM), dtype) for _ in range(chunks)
        ]
        + [
            pltpu.VMEM((n_ctx, chunk_heads, requests, slab, two, HDIM), dtype)
            for _ in range(chunks)
        ]
        + [
            dma((chunks, n_db)),
            dma((chunks, n_db)),
            dma((chunks,)),
            dma((chunks, n_ctx)),
            dma((chunks, n_ctx)),
            dma((chunks,)),
            dma((2, n_db)),
            dma((2, n_db)),
            dma,
        ],
        compiler_params=pltpu.CompilerParams(
            collective_id=0, has_side_effects=True, vmem_limit_bytes=32 * 1024 * 1024
        ),
        cost_estimate=pl.CostEstimate(
            flops=0, bytes_accessed=96 * encoded_kv.size * encoded_kv.dtype.itemsize, transcendentals=0
        ),
        name="exchange",
    )(neighbour_ids, encoded_kv, stream)


def attend_kernel(spans, q, kv, out):
    keys = kv.shape[1]
    odd = lax.rem(lax.broadcasted_iota(jnp.int32, (SPAN, keys), 1), 2) == 1
    spread = [slice(s * SPAN, (s + 1) * SPAN) for s in range(spans)]
    scores = [
        lax.dot_general(
            q[rows, :], kv[s], (((1,), (1,)), ((), ())), preferred_element_type=jnp.float32
        )
        for s, rows in enumerate(spread)
    ]
    scores = [jnp.where(odd, -jnp.inf, x * HDIM ** (-0.5)) for x in scores]
    tops = [jnp.max(x, axis=-1, keepdims=True) for x in scores]
    exponents = [jnp.exp(x - top) for x, top in zip(scores, tops)]
    sums = [1.0 / jnp.sum(x, axis=-1, keepdims=True) for x in exponents]
    weights = [pltpu.roll(x * total, 1, 1).astype(jnp.bfloat16) for x, total in zip(exponents, sums)]
    mixed = [
        jnp.dot(x, kv[s], preferred_element_type=jnp.float32) for s, x in enumerate(weights)
    ]
    for rows, x in zip(spread, mixed):
        out[rows, :] = x.astype(jnp.bfloat16)


def attend(queries, pairs):
    rows, width = queries.shape
    heads, spans, keys, _ = pairs.shape
    return pl.pallas_call(
        functools.partial(attend_kernel, spans),
        grid=(heads,),
        out_shape=jax.ShapeDtypeStruct((rows, width), jnp.bfloat16),
        in_specs=[
            pl.BlockSpec((rows, HDIM), lambda h: (0, h)),
            pl.BlockSpec((None, spans, keys, HDIM), lambda h: (h, 0, 0, 0)),
        ],
        out_specs=pl.BlockSpec((rows, HDIM), lambda h: (0, h)),
        compiler_params=pltpu.CompilerParams(vmem_limit_bytes=32 * 1024 * 1024),
        name="attend",
    )(queries, pairs)


def on_device(stream, history, dwa_weights, w_query, w_out, encoded_kv, neighbour_ids):
    tok_rows = stream.shape[0]
    local_width = w_query.shape[1]
    spans_here = tok_rows // SPAN
    lead_rows = SPAN - 1
    query_full = lax.all_gather(w_query, "ctx", axis=0, tiled=True)
    out_full = lax.all_gather(w_out, "ctx", axis=1, tiled=True)
    arrived, full_stream = exchange(encoded_kv, neighbour_ids, stream)
    queries = jnp.dot(full_stream, query_full, preferred_element_type=jnp.float32).astype(
        jnp.bfloat16
    )
    pairs = arrived.reshape(local_width // HDIM, spans_here, -1, HDIM)
    following = shifted(queries[:lead_rows], "ctx", -1)
    grouped = jnp.concatenate([queries[lead_rows:], following], 0)
    mixed = attend(grouped, pairs)
    earlier = shifted(mixed[tok_rows - lead_rows :], "ctx", 1)
    attended = jnp.concatenate([earlier, mixed[: tok_rows - lead_rows]], 0)
    partial_value = jnp.dot(attended, out_full, preferred_element_type=jnp.float32)
    summed = lax.psum_scatter(
        partial_value.astype(jnp.bfloat16), "db", scatter_dimension=1, tiled=True
    ).astype(jnp.float32)
    block = stream.astype(jnp.float32) + summed
    dense = dwa_weights[-1] * block + jnp.sum(
        history.astype(jnp.float32) * dwa_weights[:-1, None, None], axis=0
    )
    return (block.astype(jnp.bfloat16), dense.astype(jnp.bfloat16))


def solution(mesh):
    placed = (
        P("ctx", "db"),
        P(None, "ctx", "db"),
        P(),
        P("ctx", "db"),
        P("db", "ctx"),
        P("db", None, "ctx", None, None),
        P(),
    )
    return jax.shard_map(
        on_device,
        mesh=mesh,
        in_specs=placed,
        out_specs=(P("ctx", "db"), P("ctx", "db")),
        check_vma=False,
    )
```
